32 devices in a mesh: row: 8 (over y, x, core), col: 4 (over z).
Axes of the slice: x: 2, y: 2, z: 4, core: 2. Of those that a mesh axis runs over, the one named last changes fastest.
Arguments:
- queries: bfloat16 [1024, 3072], P('row'), may hold values from -30 to 30
- latent_pool: bfloat16 [128, 64, 576], P('col'), may hold values from -6 to 6
- block_table: int32 [128], P('col'), may hold values from 0 to 31, as said below
- page_len: int32 [128], P('col'), may hold values from 16 to 64
- group_offset: int32 [1], replicated, may hold values from 0 to 7168
- hidden: bfloat16 [1024, 2048], P('row'), may hold values from -4 to 4
- latent_up: bfloat16 [512, 4096], replicated, may hold values from -0.25 to 0.25
- output_weight: bfloat16 [2048, 2048], P('col'), may hold values from -0.1875 to 0.1875
- gate_weight: bfloat16 [2048, 10944], P('row', 'col'), may hold values from -0.125 to 0.125
- up_weight: bfloat16 [2048, 10944], P('row', 'col'), may hold values from -0.125 to 0.125
- down_weight: bfloat16 [10944, 2048], P('col', 'row'), may hold values from -0.078125 to 0.078125
Outputs:
- attended: bfloat16 [1024, 2048], P('row')
- block_out: bfloat16 [1024, 2048], P('row', 'col')
The draws below stay inside these ranges and needn't reach their ends.
Inputs may be any that keep to these rules, and one draw needn't show every extreme that they name: `block_table`: the 32 logical pages of one col index name its 32 pool pages, each once.
All inputs are finite; a program needn't handle non-finite values.
Results may differ from the reference program's by a relative error of at most 0.015.
Values may be sent and summed in bfloat16 or wider, within the bound.
No kernel may reach another device: no remote copies, remote signals or barrier semaphores. Data moves between devices by JAX's collectives and lax.ppermute only.
A program may use at most 128 MiB of HBM per device.

```python
import math
import jax
import jax.numpy as jnp
from jax import lax

D = 2048
H = 16
NOPE = 128
ROPE = 64
VDIM = 128
LATENT = 512
FF = 10944
PAGE = 64
PAGES_DEV = 32
QK = 192
CACHE_W = 576
Q = 1024
L = 8192
NPAGES = 128


def shared_draw(key):
    col_count = NPAGES // PAGES_DEV
    perm_keys = jax.random.split(jax.random.fold_in(key, 11), col_count)
    local_pages = jax.vmap(lambda one_key: jax.random.permutation(one_key, PAGES_DEV))(perm_keys)
    table = local_pages.reshape(NPAGES).astype(jnp.int32)
    pool_values = jnp.clip(jax.random.normal(jax.random.fold_in(key, 12), (NPAGES, PAGE, LATENT + ROPE), jnp.float32), -6.0, 6.0)
    query_values = 2.5 * jnp.clip(jax.random.normal(jax.random.fold_in(key, 13), (Q, H, QK), jnp.float32), -6.0, 6.0)
    strong_rows = jax.random.bernoulli(jax.random.fold_in(key, 20), 0.25, (Q, 1, 1))
    query_values = query_values * jnp.where(strong_rows, 4.0, 1.0)
    query_values = jnp.clip(query_values, -30.0, 30.0)
    return (table, pool_values, query_values.reshape(Q, H * QK))


def draw_queries(key, part):
    return shared_draw(key)[2].astype(jnp.bfloat16)


def draw_latent_pool(key, part):
    return shared_draw(key)[1].astype(jnp.bfloat16)


def draw_block_table(key, part):
    return shared_draw(key)[0]


def draw_page_len(key, part):
    lengths = jax.random.randint(jax.random.fold_in(key, 16), (NPAGES,), PAGE // 4, PAGE + 1).astype(jnp.int32)
    lengths = lengths.at[0].set(PAGE)
    return lengths.at[NPAGES - 1].set(PAGE // 4)


def draw_hidden(key, part):
    values = jnp.clip(jax.random.normal(jax.random.fold_in(key, 17), (Q, D), jnp.float32), -6.0, 6.0)
    trend = 3.0 ** (jnp.arange(D, dtype=jnp.float32) / D)
    col_gain = 0.02 * trend * 10.0 ** jax.random.uniform(jax.random.fold_in(key, 18), (D,), jnp.float32, 0.0, 1.0)
    values = values * col_gain[None, :]
    return values.astype(jnp.bfloat16)


def raised(result, stream_key, source, target, shards_of, factor):
    def block_of(axis_at):
        return (jnp.arange(result.shape[axis_at]) // (result.shape[axis_at] // shards_of)).reshape((-1,) + (1,) * (result.ndim - 1 - axis_at))

    near = jax.random.permutation(stream_key, shards_of)[block_of(target)]
    other_side = (block_of(target) + shards_of // 2) % shards_of
    return jnp.where((block_of(source) == near) | (block_of(source) == other_side), factor * result, result)


def shard_levels(stream_key, shape, pieces, smallest, high):
    level = 1.0
    for position, shards_of in pieces:
        draws = jax.random.uniform(jax.random.fold_in(jax.random.fold_in(stream_key, 6), position), (shards_of,), jnp.float32, smallest / len(pieces), high / len(pieces))
        level = level * jnp.repeat(jnp.exp(draws), shape[position] // shards_of).reshape((-1,) + (1,) * (len(shape) - 1 - position))
    return level


def noise(stream_key, shape, scale, reach, cuts=(), kind=jnp.bfloat16):
    entries = jax.random.normal(stream_key, shape, jnp.float32) * scale
    if len(cuts) > 0:
        entries = shard_levels(stream_key, shape, cuts, -0.22, 0.18) * entries
    return jnp.clip(entries, min=-reach, max=reach).astype(kind)


def heavy_noise(key, extent, spread, bound, shards, heavy, held_as=jnp.bfloat16):
    entries = spread * jax.random.normal(key, extent, jnp.float32)
    if shards:
        entries = entries * shard_levels(key, extent, shards, -0.22, 0.18)
    return jnp.clip(raised(entries, jax.random.fold_in(key, 3), *heavy), -bound, bound).astype(held_as)


def setup_inputs(seed: int = 0) -> dict:
    arg_keys = jax.random.split(jax.random.key(seed), 12)
    queries = draw_queries(jax.random.fold_in(arg_keys[11], 71), 0)
    latent_pool = draw_latent_pool(jax.random.fold_in(arg_keys[11], 71), 0)
    block_table = draw_block_table(jax.random.fold_in(arg_keys[11], 71), 0)
    page_len = draw_page_len(jax.random.fold_in(arg_keys[11], 71), 0)
    group_offset = jax.random.randint(arg_keys[4], (1,), 0, L - Q + 1).astype(jnp.int32)
    hidden = draw_hidden(jax.random.fold_in(arg_keys[11], 71), 0)
    latent_up = noise(arg_keys[6], (LATENT, H * (NOPE + VDIM)), LATENT ** -0.5, 0.25)
    output_weight = heavy_noise(arg_keys[7], (H * VDIM, D), (H * VDIM) ** -0.5, 0.1875, ((0, 4),), (0, 1, 4, 2.0))
    gate_weight = noise(arg_keys[8], (D, FF), D ** -0.5, 0.125, ((0, 8), (1, 4)))
    up_weight = noise(arg_keys[9], (D, FF), D ** -0.5, 0.125, ((0, 8), (1, 4)))
    down_weight = heavy_noise(arg_keys[10], (FF, D), FF ** -0.5, 0.078125, ((0, 4), (1, 8)), (0, 1, 8, 2.0))
    return {"queries": queries, "latent_pool": latent_pool, "block_table": block_table, "page_len": page_len, "group_offset": group_offset, "hidden": hidden, "latent_up": latent_up, "output_weight": output_weight, "gate_weight": gate_weight, "up_weight": up_weight, "down_weight": down_weight}


def reference(queries, latent_pool, block_table, page_len, group_offset, hidden, latent_up, output_weight, gate_weight, up_weight, down_weight):
    owners = jnp.arange(NPAGES, dtype=jnp.int32) // PAGES_DEV * PAGES_DEV
    latent = latent_pool[owners + block_table].reshape(L, CACHE_W)
    key_index = jnp.arange(L, dtype=jnp.int32)
    key_valid = key_index % PAGE < jnp.repeat(page_len, PAGE)
    query_pos = group_offset[0] + jnp.arange(Q, dtype=jnp.int32)
    per_head = queries.reshape(Q, H, QK)
    score_scale = 1.0 / math.sqrt(QK)
    block_rows = math.gcd(Q, 512)

    def one_head(head_index):
        columns = lax.dynamic_slice_in_dim(latent_up, head_index * (NOPE + VDIM), NOPE + VDIM, 1)
        expanded = jnp.dot(latent[:, :LATENT], columns, preferred_element_type=jnp.float32).astype(jnp.bfloat16)
        key_rows = jnp.concatenate([expanded[:, :NOPE], latent[:, LATENT:]], axis=1)
        values = expanded[:, NOPE:]
        head_queries = lax.dynamic_index_in_dim(per_head, head_index, 1, keepdims=False)

        def one_block(block_index):
            block_queries = lax.dynamic_slice_in_dim(head_queries, block_index * block_rows, block_rows, 0)
            block_pos = lax.dynamic_slice_in_dim(query_pos, block_index * block_rows, block_rows, 0)
            scores = jnp.dot(block_queries, key_rows.T, preferred_element_type=jnp.float32) * score_scale
            visible = key_valid[None, :] & (key_index[None, :] <= block_pos[:, None])
            row_max = lax.optimization_barrier(jnp.max(jnp.where(visible, scores, -jnp.inf), axis=1, keepdims=True))
            weights = jnp.where(visible, jnp.exp(scores - row_max), 0.0)
            weighted = jnp.dot(weights.astype(jnp.bfloat16), values, preferred_element_type=jnp.float32)
            return (weighted / lax.optimization_barrier(jnp.sum(weights, axis=1, keepdims=True))).astype(jnp.bfloat16)
        blocks = lax.map(one_block, jnp.arange(Q // block_rows, dtype=jnp.int32))
        return blocks.reshape(Q, VDIM)
    head_outputs = lax.map(one_head, jnp.arange(H, dtype=jnp.int32))
    head_mix = jnp.transpose(head_outputs, (1, 0, 2)).reshape(Q, H * VDIM)
    projected = jnp.dot(head_mix, output_weight, preferred_element_type=jnp.float32)
    attended = (hidden.astype(jnp.float32) + projected).astype(jnp.bfloat16)
    wide = attended.astype(jnp.float32)
    mean_square = lax.optimization_barrier(jnp.mean(wide * wide, axis=1, keepdims=True))
    normed = (wide * lax.rsqrt(mean_square + 1e-06)).astype(jnp.bfloat16)
    gate_sum = jnp.dot(normed, gate_weight, preferred_element_type=jnp.float32)
    up_sum = jnp.dot(normed, up_weight, preferred_element_type=jnp.float32)
    activated = (jax.nn.silu(gate_sum) * up_sum).astype(jnp.bfloat16)
    mlp_terms = jnp.dot(activated, down_weight, preferred_element_type=jnp.float32)
    block_out = (wide + mlp_terms).astype(jnp.bfloat16)
    return (attended, block_out)
```

```python
import functools
import math

import jax
import jax.numpy as jnp
from jax import lax
from jax.experimental import pallas as pl
from jax.experimental.pallas import tpu as pltpu
from jax.sharding import PartitionSpec as P

H = 16
NOPE = 128
ROPE = 64
VDIM = 128
LATENT = 512
QK = NOPE + ROPE
HEAD_UP = NOPE + VDIM
LANES = 128
TAIL = 16
HIDDEN_SCORE = -1e30
LOG2_SCALE = math.log2(math.e) / math.sqrt(QK)
NT = (((1,), (1,)), ((), ()))


def exchange(x, axis, step):
    count = lax.axis_size(axis)
    return lax.ppermute(x, axis, [(i, i ^ step) for i in range(count)])


def rotate(x, axis, step):
    count = lax.axis_size(axis)
    return lax.ppermute(x, axis, [(i, (i + step) % count) for i in range(count)])


def attention_kernel(
    groups, table_ref, len_ref, meta_ref, queries_ref, pool_ref, up_ref, *refs
):
    outs = refs[:groups]
    pages_ref, keys_ref, q_ref, sem = refs[groups:]
    page_count, page_size, _ = pages_ref.shape
    query_rows = queries_ref.shape[0]
    heads_here = H // groups
    first_query = meta_ref[0]
    first_key = meta_ref[1]
    col_index = meta_ref[2]

    def page_copy(p):
        return pltpu.make_async_copy(pool_ref.at[table_ref[p]], pages_ref.at[p], sem.at[p])

    for p in range(page_count):
        page_copy(p).start()

    eye = (
        lax.broadcasted_iota(jnp.int32, (query_rows, query_rows), 0)
        == lax.broadcasted_iota(jnp.int32, (query_rows, query_rows), 1)
    ).astype(jnp.bfloat16)
    for h in range(H):
        rows = pl.ds(h * query_rows, query_rows)
        q_nope = queries_ref[:, h * QK : h * QK + NOPE]
        up_k = up_ref[:, h * HEAD_UP : h * HEAD_UP + NOPE]
        absorbed = lax.dot_general(q_nope, up_k, NT, preferred_element_type=jnp.float32)
        q_ref[rows, :LATENT] = absorbed.astype(jnp.bfloat16)
        q_rope = queries_ref[:, h * QK + NOPE : (h + 1) * QK]
        q_ref[rows, LATENT : LATENT + LANES] = jnp.concatenate(
            [q_rope, jnp.zeros((query_rows, LANES - ROPE), jnp.bfloat16)], axis=1
        )
        q_ref[rows, LATENT + LANES :] = eye

    slot = lax.broadcasted_iota(jnp.int32, (page_size, query_rows), 0)
    query_pos = first_query + lax.broadcasted_iota(jnp.int32, (page_size, query_rows), 1)
    for p in range(page_count):
        page_copy(p).wait()
        rows = pl.ds(p * page_size, page_size)
        page = pages_ref[p]
        keys_ref[rows, :LATENT] = page[:, :LATENT]
        keys_ref[rows, LATENT : LATENT + LANES] = jnp.concatenate(
            [page[:, LATENT:], jnp.zeros((page_size, LANES - ROPE), jnp.bfloat16)], axis=1
        )
        seen = (slot < len_ref[p]) & (first_key + p * page_size + slot <= query_pos)
        keys_ref[rows, LATENT + LANES :] = jnp.where(seen, 0.0, HIDDEN_SCORE).astype(jnp.bfloat16)

    for step in range(groups):
        group = lax.rem(col_index + step, groups)
        block = heads_here * query_rows
        q_rows = q_ref[pl.ds(pl.multiple_of(group * block, block), block), :]
        scores = lax.dot_general(q_rows, keys_ref[...], NT, preferred_element_type=jnp.float32)
        row_max = jnp.max(scores, axis=1, keepdims=True)
        weights = jnp.exp2((scores - row_max) * LOG2_SCALE)
        totals = jnp.sum(weights, axis=1, keepdims=True)
        context = jnp.dot(
            weights.astype(jnp.bfloat16), keys_ref[:, :LATENT], preferred_element_type=jnp.float32
        )
        context = (context / totals).astype(jnp.bfloat16)
        log_sum = row_max * LOG2_SCALE + jnp.log2(totals)
        out_ref = outs[step]
        tail = []
        for j in range(heads_here):
            own = slice(j * query_rows, (j + 1) * query_rows)
            at = pl.multiple_of((group * heads_here + j) * HEAD_UP + NOPE, LANES)
            up_v = up_ref[:, pl.ds(at, VDIM)]
            mixed = jnp.dot(context[own], up_v, preferred_element_type=jnp.float32)
            out_ref[:query_rows, j * VDIM : (j + 1) * VDIM] = mixed.astype(jnp.bfloat16)
            wide = jnp.broadcast_to(log_sum[own], (query_rows, LANES))
            tail.append(jnp.transpose(wide)[:1])
        tail = jnp.concatenate(tail, axis=1)
        high = tail.astype(jnp.bfloat16)
        rest = tail - high.astype(jnp.float32)
        middle = rest.astype(jnp.bfloat16)
        low = (rest - middle.astype(jnp.float32)).astype(jnp.bfloat16)
        width = tail.shape[1]
        parts = [high.astype(jnp.float32), middle.astype(jnp.float32), low.astype(jnp.float32)]
        parts.append(jnp.zeros((TAIL - 3, width), jnp.float32))
        out_ref[query_rows:, :] = jnp.concatenate(parts, axis=0).astype(jnp.bfloat16)


def attention(queries, latent_pool, block_table, page_len, latent_up, meta, groups):
    query_rows = queries.shape[0]
    page_count, page_size, cache_width = latent_pool.shape
    keys = page_count * page_size
    width = LATENT + LANES + query_rows
    heads_here = H // groups
    vmem = pl.BlockSpec(memory_space=pltpu.VMEM)
    smem = pl.BlockSpec(memory_space=pltpu.SMEM)
    payload = jax.ShapeDtypeStruct((query_rows + TAIL, heads_here * VDIM), jnp.bfloat16)
    return pl.pallas_call(
        functools.partial(attention_kernel, groups),
        out_shape=[payload] * groups,
        in_specs=[smem, smem, smem, vmem, pl.BlockSpec(memory_space=pl.ANY), vmem],
        out_specs=[vmem] * groups,
        scratch_shapes=[
            pltpu.VMEM((page_count, page_size, cache_width), jnp.bfloat16),
            pltpu.VMEM((keys, width), jnp.bfloat16),
            pltpu.VMEM((H * query_rows, width), jnp.bfloat16),
            pltpu.SemaphoreType.DMA((page_count,)),
        ],
        compiler_params=pltpu.CompilerParams(vmem_limit_bytes=48 * 1024 * 1024),
        cost_estimate=pl.CostEstimate(
            flops=2 * H * query_rows * keys * (width + LATENT),
            bytes_accessed=16 * 1024 * 1024,
            transcendentals=H * query_rows * keys,
        ),
        name="attention",
    )(block_table, page_len, meta, queries, latent_pool, latent_up)


def project_kernel(groups, meta_ref, weight_ref, *refs):
    parts, outs = refs[:groups], refs[groups:]
    query_rows = outs[0].shape[0]
    width = outs[0].shape[1]
    heads_here = parts[0].shape[1] // VDIM
    col_index = meta_ref[2]
    mixed = []
    for j in range(heads_here):
        lanes = slice(j * VDIM, (j + 1) * VDIM)
        logs = []
        for part in parts:
            tail = part[query_rows:, lanes].astype(jnp.float32)
            line = tail[0:1] + tail[1:2] + tail[2:3]
            logs.append(jnp.transpose(jnp.broadcast_to(line, (LANES, query_rows))))
        top = functools.reduce(jnp.maximum, logs)
        scales = [jnp.exp2(v - top) for v in logs]
        total = functools.reduce(jnp.add, scales)
        value = functools.reduce(
            jnp.add, [s * part[:query_rows, lanes].astype(jnp.float32) for s, part in zip(scales, parts)]
        )
        mixed.append((value / total).astype(jnp.bfloat16))
    mixed = jnp.concatenate(mixed, axis=1)
    for step in range(groups):
        at = pl.multiple_of(lax.rem(col_index + step, groups) * width, width)
        columns = weight_ref[:, pl.ds(at, width)]
        outs[step][...] = jnp.dot(mixed, columns, preferred_element_type=jnp.float32).astype(
            jnp.bfloat16
        )


def project(parts, output_weight, meta, query_rows):
    groups = len(parts)
    vmem = pl.BlockSpec(memory_space=pltpu.VMEM)
    width = output_weight.shape[1] // groups
    return pl.pallas_call(
        functools.partial(project_kernel, groups),
        out_shape=[jax.ShapeDtypeStruct((query_rows, width), jnp.bfloat16)] * groups,
        in_specs=[pl.BlockSpec(memory_space=pltpu.SMEM)] + [vmem] * (1 + groups),
        out_specs=[vmem] * groups,
        compiler_params=pltpu.CompilerParams(vmem_limit_bytes=32 * 1024 * 1024),
        name="project",
    )(meta, output_weight, *parts)


def on_device(
    queries,
    latent_pool,
    block_table,
    page_len,
    group_offset,
    hidden,
    latent_up,
    output_weight,
    gate_weight,
    up_weight,
    down_weight,
):
    cols = lax.axis_size("col")
    chips = lax.axis_size("row") // 2
    col_index = lax.axis_index("col")
    row_index = lax.axis_index("row")
    chip_index = row_index // 2
    core_index = row_index % 2
    query_rows, model = hidden.shape
    keys_here = latent_pool.shape[0] * latent_pool.shape[1]
    depth, units = gate_weight.shape
    share = -(-units // (chips * LANES)) * LANES
    width = model // cols

    pad = chips * share - units
    gate_padded = jnp.pad(gate_weight, ((0, 0), (0, pad)))
    up_padded = jnp.pad(up_weight, ((0, 0), (0, pad)))
    down_padded = jnp.pad(down_weight, ((0, pad), (0, 0)))
    ins, downs = [], []
    for step in range(chips):
        at = (chip_index ^ step) * share
        gate_up = jnp.concatenate(
            [
                lax.dynamic_slice_in_dim(gate_padded, at, share, 1),
                lax.dynamic_slice_in_dim(up_padded, at, share, 1),
            ],
            axis=0,
        )
        down = lax.dynamic_slice_in_dim(down_padded, at, share, 0)
        ins.append(exchange(gate_up, "row", 2 * step) if step else gate_up)
        downs.append(exchange(down, "row", 2 * step) if step else down)
    ins = jnp.stack(ins)
    downs = jnp.stack(downs)
    ins = jnp.stack([ins, exchange(ins, "row", 1)])
    downs = jnp.stack([downs, exchange(downs, "row", 1)])
    order = jnp.arange(chips, dtype=jnp.int32) ^ chip_index
    cores = jnp.arange(2, dtype=jnp.int32) ^ core_index
    ins = ins[cores[None, :], order[:, None]].reshape(2 * chips, 2, depth, share)
    gate_all = ins[:, 0].reshape(model, share)
    up_all = ins[:, 1].reshape(model, share)
    downs = downs[cores[None, :], order[:, None]].reshape(2 * chips, share, depth)
    down_all = downs.transpose(1, 0, 2).reshape(share, model)

    meta = jnp.stack(
        [group_offset[0] + row_index * query_rows, col_index * keys_here, col_index]
    ).astype(jnp.int32)
    payloads = attention(queries, latent_pool, block_table, page_len, latent_up, meta, cols)
    parts = [payloads[0]] + [rotate(payloads[s], "col", s) for s in range(1, cols)]
    terms = project(parts, output_weight, meta, query_rows)
    here = lax.dynamic_slice_in_dim(hidden, col_index * width, width, 1).astype(jnp.float32)
    here = here + terms[0].astype(jnp.float32)
    for s in range(1, cols):
        here = here + rotate(terms[s], "col", s).astype(jnp.float32)
    here = here.astype(jnp.bfloat16)
    pieces = jnp.stack([here] + [rotate(here, "col", s) for s in range(1, cols)])
    col_order = (col_index - jnp.arange(cols, dtype=jnp.int32)) % cols
    attended = pieces[col_order].transpose(1, 0, 2).reshape(query_rows, model)

    wide = attended.astype(jnp.float32)
    mean_square = jnp.mean(wide * wide, axis=1, keepdims=True)
    normed = (wide * lax.rsqrt(mean_square + 1e-06)).astype(jnp.bfloat16)
    tokens = jnp.concatenate(
        [normed] + [exchange(normed, "row", 2 * s) for s in range(1, chips)], axis=0
    )
    gate_sum = jnp.dot(tokens, gate_all, preferred_element_type=jnp.float32)
    up_sum = jnp.dot(tokens, up_all, preferred_element_type=jnp.float32)
    activated = (jax.nn.silu(gate_sum) * up_sum).astype(jnp.bfloat16)
    out = jnp.dot(activated, down_all, preferred_element_type=jnp.float32).astype(jnp.bfloat16)
    out = out.reshape(chips, query_rows, model)
    summed = out[0].astype(jnp.float32)
    for s in range(1, chips):
        summed = summed + exchange(out[s], "row", 2 * s).astype(jnp.float32)

    def chunk(s):
        at = ((col_index + s) % cols) * width
        return lax.dynamic_slice_in_dim(summed, at, width, 1)

    total = here.astype(jnp.float32) + chunk(0)
    for s in range(1, cols):
        total = total + rotate(chunk(s).astype(jnp.bfloat16), "col", s).astype(jnp.float32)
    return (attended, total.astype(jnp.bfloat16))


def solution(mesh):
    placed = (
        P("row", None),
        P("col", None, None),
        P("col"),
        P("col"),
        P(),
        P("row", None),
        P(),
        P("col", None),
        P("row", "col"),
        P("row", "col"),
        P("col", "row"),
    )
    return jax.shard_map(
        on_device,
        mesh=mesh,
        in_specs=placed,
        out_specs=(P("row", None), P("row", "col")),
        check_vma=False,
    )
```

```python
import functools
import math

import jax
import jax.numpy as jnp
from jax import lax
from jax.experimental import pallas as pl
from jax.experimental.pallas import tpu as pltpu
from jax.sharding import PartitionSpec as P

H = 16
NOPE = 128
ROPE = 64
VDIM = 128
LATENT = 512
QK = NOPE + ROPE
HEAD_UP = NOPE + VDIM
LANES = 128
TAIL = 16
HIDDEN_SCORE = -1e30
VMEM_LIMIT = 24 * 1024 * 1024
PREPARE_LIMIT = 12 * 1024 * 1024
SUBLANES = 16
META = 6
LOG2_SCALE = math.log2(math.e) / math.sqrt(QK)
NT = (((1,), (1,)), ((), ()))


def exchange(x, axis, step):
    count = lax.axis_size(axis)
    return lax.ppermute(x, axis, [(i, i ^ step) for i in range(count)])


def rotate(x, axis, step):
    count = lax.axis_size(axis)
    return lax.ppermute(x, axis, [(i, (i + step) % count) for i in range(count)])


def rows_of(ref, index, size):
    return ref[pl.ds(pl.multiple_of(index * size, size), size), :]


def prepare_kernel(
    chips, meta_ref, queries_hbm, pool_hbm, up_hbm, gate_hbm, unit_hbm, down_hbm, *refs
):
    q_ref, keys_ref, up_ref = refs[:3]
    shares, refs = refs[3 : 3 + chips], refs[3 + chips :]
    pages_ref, queries_ref, page_sem, share_sem, sem = refs
    page_count, page_size, _ = pages_ref.shape
    query_rows = queries_ref.shape[0]
    first_query = meta_ref[0]
    first_key = meta_ref[1]
    share = shares[0].shape[0] // 3
    table_at = META + chips
    len_at = table_at + page_count

    queries_copy = pltpu.make_async_copy(queries_hbm, queries_ref, sem.at[0])
    up_copy = pltpu.make_async_copy(up_hbm, up_ref, sem.at[1])
    page_copies = [
        pltpu.make_async_copy(pool_hbm.at[meta_ref[table_at + p]], pages_ref.at[p], page_sem.at[p])
        for p in range(page_count)
    ]
    share_copies = []
    for step in range(chips):
        rows = pl.ds(pl.multiple_of(meta_ref[META + step], SUBLANES), share)
        for i, source in enumerate((gate_hbm, unit_hbm, down_hbm)):
            target = shares[step].at[pl.ds(i * share, share), :]
            share_copies.append(
                pltpu.make_async_copy(source.at[rows, :], target, share_sem.at[3 * step + i])
            )
    for copy in page_copies + [queries_copy, up_copy] + share_copies:
        copy.start()

    slot = lax.broadcasted_iota(jnp.int32, (page_size, query_rows), 0)
    query_pos = first_query + lax.broadcasted_iota(jnp.int32, (page_size, query_rows), 1)
    for p in range(page_count):
        page_copies[p].wait()
        rows = pl.ds(p * page_size, page_size)
        page = pages_ref[p]
        keys_ref[rows, :LATENT] = page[:, :LATENT]
        keys_ref[rows, LATENT : LATENT + LANES] = jnp.concatenate(
            [page[:, LATENT:], jnp.zeros((page_size, LANES - ROPE), jnp.bfloat16)], axis=1
        )
        seen = (slot < meta_ref[len_at + p]) & (first_key + p * page_size + slot <= query_pos)
        keys_ref[rows, LATENT + LANES :] = jnp.where(seen, 0.0, HIDDEN_SCORE).astype(jnp.bfloat16)

    eye = (
        lax.broadcasted_iota(jnp.int32, (query_rows, query_rows), 0)
        == lax.broadcasted_iota(jnp.int32, (query_rows, query_rows), 1)
    ).astype(jnp.bfloat16)
    queries_copy.wait()
    up_copy.wait()
    for h in range(H):
        rows = pl.ds(h * query_rows, query_rows)
        q_nope = queries_ref[:, h * QK : h * QK + NOPE]
        up_k = up_ref[:, h * HEAD_UP : h * HEAD_UP + NOPE]
        absorbed = lax.dot_general(q_nope, up_k, NT, preferred_element_type=jnp.float32)
        q_ref[rows, :LATENT] = absorbed.astype(jnp.bfloat16)
        q_rope = queries_ref[:, h * QK + NOPE : (h + 1) * QK]
        q_ref[rows, LATENT : LATENT + LANES] = jnp.concatenate(
            [q_rope, jnp.zeros((query_rows, LANES - ROPE), jnp.bfloat16)], axis=1
        )
        q_ref[rows, LATENT + LANES :] = eye
    for copy in share_copies:
        copy.wait()


def prepare(queries, latent_pool, latent_up, by_unit, meta, chips, share):
    query_rows = queries.shape[0]
    page_count, page_size, cache_width = latent_pool.shape
    keys = page_count * page_size
    width = LATENT + LANES + query_rows
    vmem = pl.BlockSpec(memory_space=pltpu.VMEM)
    smem = pl.BlockSpec(memory_space=pltpu.SMEM)
    hbm = pl.BlockSpec(memory_space=pltpu.HBM)
    sources = (queries, latent_pool, latent_up, *by_unit)
    out = pl.pallas_call(
        functools.partial(prepare_kernel, chips),
        out_shape=[
            pltpu.VMEM((H * query_rows, width), jnp.bfloat16),
            pltpu.VMEM((keys, width), jnp.bfloat16),
            pltpu.VMEM(latent_up.shape, jnp.bfloat16),
        ]
        + [pltpu.VMEM((3 * share, by_unit[0].shape[1]), jnp.bfloat16)] * chips,
        in_specs=[smem] + [hbm] * 6,
        out_specs=[vmem] * (3 + chips),
        scratch_shapes=[
            pltpu.VMEM((page_count, page_size, cache_width), jnp.bfloat16),
            pltpu.VMEM(queries.shape, jnp.bfloat16),
            pltpu.SemaphoreType.DMA((page_count,)),
            pltpu.SemaphoreType.DMA((3 * chips,)),
            pltpu.SemaphoreType.DMA((2,)),
        ],
        compiler_params=pltpu.CompilerParams(vmem_limit_bytes=PREPARE_LIMIT),
        cost_estimate=pl.CostEstimate(flops=0, bytes_accessed=0, transcendentals=0),
        name="prepare",
    )(meta, *[pltpu.with_memory_space_constraint(x, pltpu.HBM) for x in sources])
    return out[0], out[1], out[2], out[3:]


def attend_kernel(step, groups, meta_ref, q_ref, keys_ref, up_ref, out_ref):
    heads_here = H // groups
    query_rows = q_ref.shape[0] // H
    group = lax.rem(meta_ref[2] + step, groups)
    q_rows = rows_of(q_ref, group, heads_here * query_rows)
    scores = lax.dot_general(q_rows, keys_ref[...], NT, preferred_element_type=jnp.float32)
    row_max = jnp.max(scores, axis=1, keepdims=True)
    weights = jnp.exp2((scores - row_max) * LOG2_SCALE)
    totals = jnp.sum(weights, axis=1, keepdims=True)
    context = jnp.dot(
        weights.astype(jnp.bfloat16), keys_ref[:, :LATENT], preferred_element_type=jnp.float32
    )
    context = (context / totals).astype(jnp.bfloat16)
    log_sum = row_max * LOG2_SCALE + jnp.log2(totals)
    tail = []
    for j in range(heads_here):
        own = slice(j * query_rows, (j + 1) * query_rows)
        at = pl.multiple_of((group * heads_here + j) * HEAD_UP + NOPE, LANES)
        up_v = up_ref[:, pl.ds(at, VDIM)]
        mixed = jnp.dot(context[own], up_v, preferred_element_type=jnp.float32)
        out_ref[:query_rows, j * VDIM : (j + 1) * VDIM] = mixed.astype(jnp.bfloat16)
        wide = jnp.broadcast_to(log_sum[own], (query_rows, LANES))
        tail.append(jnp.transpose(wide)[:1])
    tail = jnp.concatenate(tail, axis=1)
    high = tail.astype(jnp.bfloat16)
    rest = tail - high.astype(jnp.float32)
    middle = rest.astype(jnp.bfloat16)
    low = (rest - middle.astype(jnp.float32)).astype(jnp.bfloat16)
    parts = [high.astype(jnp.float32), middle.astype(jnp.float32), low.astype(jnp.float32)]
    parts.append(jnp.zeros((TAIL - 3, tail.shape[1]), jnp.float32))
    out_ref[query_rows:, :] = jnp.concatenate(parts, axis=0).astype(jnp.bfloat16)


def attend(step, groups, meta, q, keys, latent_up):
    query_rows = q.shape[0] // H
    heads_here = H // groups
    vmem = pl.BlockSpec(memory_space=pltpu.VMEM)
    return pl.pallas_call(
        functools.partial(attend_kernel, step, groups),
        out_shape=jax.ShapeDtypeStruct((query_rows + TAIL, heads_here * VDIM), jnp.bfloat16),
        in_specs=[pl.BlockSpec(memory_space=pltpu.SMEM), vmem, vmem, vmem],
        out_specs=vmem,
        compiler_params=pltpu.CompilerParams(vmem_limit_bytes=VMEM_LIMIT),
        cost_estimate=pl.CostEstimate(
            flops=2 * heads_here * query_rows * keys.shape[0] * (keys.shape[1] + LATENT),
            bytes_accessed=4 * 1024 * 1024,
            transcendentals=heads_here * query_rows * keys.shape[0],
        ),
        name="attend",
    )(meta, q, keys, latent_up)


def project_kernel(groups, meta_ref, weight_ref, *refs):
    parts, outs = refs[:groups], refs[groups:]
    query_rows = outs[0].shape[0]
    width = outs[0].shape[1]
    heads_here = parts[0].shape[1] // VDIM
    col_index = meta_ref[2]
    mixed = []
    for j in range(heads_here):
        lanes = slice(j * VDIM, (j + 1) * VDIM)
        logs = []
        for part in parts:
            tail = part[query_rows:, lanes].astype(jnp.float32)
            line = tail[0:1] + tail[1:2] + tail[2:3]
            logs.append(jnp.transpose(jnp.broadcast_to(line, (LANES, query_rows))))
        top = functools.reduce(jnp.maximum, logs)
        scales = [jnp.exp2(v - top) for v in logs]
        total = functools.reduce(jnp.add, scales)
        value = functools.reduce(
            jnp.add, [s * part[:query_rows, lanes].astype(jnp.float32) for s, part in zip(scales, parts)]
        )
        mixed.append((value / total).astype(jnp.bfloat16))
    mixed = jnp.concatenate(mixed, axis=1)
    for step in range(groups):
        at = pl.multiple_of(lax.rem(col_index + step, groups) * width, width)
        columns = weight_ref[:, pl.ds(at, width)]
        outs[step][...] = jnp.dot(mixed, columns, preferred_element_type=jnp.float32).astype(
            jnp.bfloat16
        )


def project(parts, output_weight, meta, query_rows):
    groups = len(parts)
    vmem = pl.BlockSpec(memory_space=pltpu.VMEM)
    width = output_weight.shape[1] // groups
    return pl.pallas_call(
        functools.partial(project_kernel, groups),
        out_shape=[jax.ShapeDtypeStruct((query_rows, width), jnp.bfloat16)] * groups,
        in_specs=[pl.BlockSpec(memory_space=pltpu.SMEM)] + [vmem] * (1 + groups),
        out_specs=[vmem] * groups,
        compiler_params=pltpu.CompilerParams(vmem_limit_bytes=32 * 1024 * 1024),
        name="project",
    )(meta, output_weight, *parts)


def assemble_kernel(chips, meta_ref, *refs):
    blocks, (out_ref, sem) = refs[: 2 * chips], refs[2 * chips :]
    depth = blocks[0].shape[1]
    chip_index, core_index = meta_ref[3], meta_ref[4]
    copies = []
    for core_step in range(2):
        for step in range(chips):
            place = 2 * (chip_index ^ step) + (core_index ^ core_step)
            lanes = pl.ds(pl.multiple_of(place * depth, depth), depth)
            number = core_step * chips + step
            copies.append(
                pltpu.make_async_copy(blocks[number], out_ref.at[:, lanes], sem.at[number])
            )
    for copy in copies:
        copy.start()
    for copy in copies:
        copy.wait()


def assemble(blocks, meta):
    rows, depth = blocks[0].shape
    anywhere = pl.BlockSpec(memory_space=pl.ANY)
    return pl.pallas_call(
        functools.partial(assemble_kernel, len(blocks) // 2),
        out_shape=jax.ShapeDtypeStruct((rows, depth * len(blocks)), blocks[0].dtype),
        in_specs=[pl.BlockSpec(memory_space=pltpu.SMEM)] + [anywhere] * len(blocks),
        out_specs=pl.BlockSpec(memory_space=pltpu.VMEM),
        scratch_shapes=[pltpu.SemaphoreType.DMA((len(blocks),))],
        compiler_params=pltpu.CompilerParams(vmem_limit_bytes=VMEM_LIMIT),
        cost_estimate=pl.CostEstimate(
            flops=0, bytes_accessed=4 * rows * depth * len(blocks), transcendentals=0
        ),
        name="assemble",
    )(meta, *blocks)


def feed_kernel(groups, chips, order, meta_ref, weights_ref, *refs):
    tokens, refs = refs[:groups], refs[groups:]
    keeps, sends, (tokens_ref, active_ref) = refs[:groups], refs[groups : 2 * groups], refs[2 * groups :]
    width = tokens[0].shape[1]
    rows, model = tokens_ref.shape
    share = active_ref.shape[1]
    query_rows = rows // chips
    col_index = meta_ref[2]
    squares = jnp.zeros((rows, 1), jnp.float32)
    for s in range(groups):
        piece = tokens[s][...]
        at = pl.multiple_of(lax.rem(col_index + groups - s, groups) * width, width)
        tokens_ref[:, pl.ds(at, width)] = piece
        wide = piece.astype(jnp.float32)
        squares = squares + jnp.sum(wide * wide, axis=1, keepdims=True)
    scale = lax.rsqrt(squares / model + 1e-06)
    gate = lax.dot_general(
        tokens_ref[...], weights_ref[:share, :], NT, preferred_element_type=jnp.float32
    )
    up = lax.dot_general(
        tokens_ref[...], weights_ref[share : 2 * share, :], NT, preferred_element_type=jnp.float32
    )
    gate = gate * scale
    active = gate / (1.0 + jnp.exp(-gate)) * (up * scale)
    unit = lax.broadcasted_iota(jnp.int32, active.shape, 1)
    active_ref[...] = jnp.where(unit < meta_ref[5], 0.0, active).astype(jnp.bfloat16)
    for s in range(groups):
        at = pl.multiple_of(lax.rem(col_index + s, groups) * width, width)
        out = jnp.dot(
            active_ref[...],
            weights_ref[2 * share :, pl.ds(at, width)],
            preferred_element_type=jnp.float32,
        ).astype(jnp.bfloat16)
        kept, sent = halves(order[s], chips)
        for ref, steps in ((keeps[s], kept), (sends[s], sent)):
            for i, step in enumerate(steps):
                ref[i * query_rows : (i + 1) * query_rows, :] = out[
                    step * query_rows : (step + 1) * query_rows
                ]


def halves(bits, chips):
    if not bits:
        return [0], []
    return [s for s in range(chips) if not s & bits[0]], [s for s in range(chips) if s & bits[0]]


def feed(weights, tokens, meta, chips, order):
    groups = len(tokens)
    rows, width = tokens[0].shape
    share = weights.shape[0] // 3
    vmem = pl.BlockSpec(memory_space=pltpu.VMEM)
    kept, sent = halves(order[0], chips)
    query_rows = rows // chips
    shapes = [
        jax.ShapeDtypeStruct((max(len(steps), 1) * query_rows, width), jnp.bfloat16)
        for steps in (kept, sent)
    ]
    return pl.pallas_call(
        functools.partial(feed_kernel, groups, chips, order),
        out_shape=[shapes[0]] * groups + [shapes[1]] * groups,
        in_specs=[pl.BlockSpec(memory_space=pltpu.SMEM)] + [vmem] * (1 + groups),
        out_specs=[vmem] * (2 * groups),
        scratch_shapes=[
            pltpu.VMEM((rows, width * groups), jnp.bfloat16),
            pltpu.VMEM((rows, share), jnp.bfloat16),
        ],
        compiler_params=pltpu.CompilerParams(vmem_limit_bytes=VMEM_LIMIT),
        cost_estimate=pl.CostEstimate(
            flops=6 * rows * width * groups * share,
            bytes_accessed=6 * share * width * groups,
            transcendentals=rows * share,
        ),
        name="feed",
    )(meta, weights, *tokens)


def gather_rows(block, bits):
    query_rows = block.shape[0]
    steps = [0]
    for bit in bits:
        block = jnp.concatenate([block, exchange(block, "row", 2 * bit)], axis=0)
        steps = steps + [s ^ bit for s in steps]
    pieces = [block[steps.index(s) * query_rows :][:query_rows] for s in range(len(steps))]
    return block if steps == sorted(steps) else jnp.concatenate(pieces, axis=0)


def sum_rows(kept, sent, bits, query_rows):
    for i, bit in enumerate(bits):
        kept = kept.astype(jnp.float32) + exchange(sent, "row", 2 * bit).astype(jnp.float32)
        if i + 1 == len(bits):
            break
        left = [s for s in range(1 << len(bits)) if not any(s & b for b in bits[: i + 1])]
        pick = [
            [n for n, s in enumerate(left) if bool(s & bits[i + 1]) == away] for away in (False, True)
        ]
        kept, sent = [
            jnp.concatenate([kept[n * query_rows : (n + 1) * query_rows] for n in rows], axis=0)
            for rows in pick
        ]
        sent = sent.astype(jnp.bfloat16)
    return kept.astype(jnp.float32)


def on_device(
    queries,
    latent_pool,
    block_table,
    page_len,
    group_offset,
    hidden,
    latent_up,
    output_weight,
    gate_weight,
    up_weight,
    down_weight,
):
    cols = lax.axis_size("col")
    chips = lax.axis_size("row") // 2
    col_index = lax.axis_index("col")
    row_index = lax.axis_index("row")
    chip_index = row_index // 2
    core_index = row_index % 2
    query_rows, model = hidden.shape
    keys_here = latent_pool.shape[0] * latent_pool.shape[1]
    depth, units = gate_weight.shape
    by_unit = (gate_weight.T, up_weight.T, down_weight)
    if units % SUBLANES:
        by_unit = [jnp.pad(w, ((0, -units % SUBLANES), (0, 0))) for w in by_unit]
        units = by_unit[0].shape[0]
    share = -(-units // (chips * SUBLANES)) * SUBLANES
    width = model // cols

    def start_of(chip):
        return jnp.minimum(chip * share, units - share)

    meta = jnp.stack(
        [
            group_offset[0] + row_index * query_rows,
            col_index * keys_here,
            col_index,
            chip_index,
            core_index,
            chip_index * share - start_of(chip_index),
        ]
        + [start_of(chip_index ^ step) for step in range(chips)]
    ).astype(jnp.int32)
    meta = jnp.concatenate([meta, block_table, page_len])
    q, keys, up_here, shares = prepare(
        queries, latent_pool, latent_up, by_unit, meta, chips, share
    )
    early = range(1, chips // 2 + 1)
    late = range(chips // 2 + 1, chips)
    blocks = {s: exchange(shares[s], "row", 2 * s) for s in early}
    swapped = {0: exchange(shares[0], "row", 1)}

    payloads = [attend(s, cols, meta, q, keys, up_here) for s in range(cols)]
    parts = [payloads[0]] + [rotate(payloads[s], "col", s) for s in range(1, cols)]
    parts, blocks, swapped, later = lax.optimization_barrier(
        (parts, blocks, swapped, [shares[s] for s in late])
    )
    for s, share_out in zip(late, later):
        blocks[s] = exchange(share_out, "row", 2 * s)
    terms = project(parts, output_weight, meta, query_rows)
    for s in early:
        swapped[s] = exchange(blocks[s], "row", 1)
    here = lax.dynamic_slice_in_dim(hidden, col_index * width, width, 1).astype(jnp.float32)
    here = here + terms[0].astype(jnp.float32)
    for s in range(1, cols):
        here = here + rotate(terms[s], "col", s).astype(jnp.float32)
    here = here.astype(jnp.bfloat16)
    here, swapped = lax.optimization_barrier((here, swapped))
    for s in late:
        swapped[s] = exchange(blocks[s], "row", 1)
    blocks[0] = shares[0]
    blocks = [blocks[s] for s in range(chips)] + [swapped[s] for s in range(chips)]
    pieces = [here] + [rotate(here, "col", s) for s in range(1, cols)]
    attended = jnp.zeros((query_rows, model), jnp.bfloat16)
    for s in range(cols):
        at = ((col_index + cols - s) % cols) * width
        attended = lax.dynamic_update_slice_in_dim(attended, pieces[s], at, 1)

    rising = [1 << i for i in range(chips.bit_length() - 1)]
    order = [rising if s % 2 == 0 else rising[::-1] for s in range(cols)]
    tokens = [gather_rows(pieces[s], order[s]) for s in range(cols)]
    out = feed(assemble(blocks, meta), tokens, meta, chips, order)
    total = here.astype(jnp.float32)
    for s in list(range(1, cols)) + [0]:
        term = sum_rows(out[s], out[cols + s], order[s], query_rows)
        if s:
            term = rotate(term.astype(jnp.bfloat16), "col", s).astype(jnp.float32)
        total = total + term
    return (attended, total.astype(jnp.bfloat16))


def solution(mesh):
    placed = (
        P("row", None),
        P("col", None, None),
        P("col"),
        P("col"),
        P(),
        P("row", None),
        P(),
        P("col", None),
        P("row", "col"),
        P("row", "col"),
        P("col", "row"),
    )
    return jax.shard_map(
        on_device,
        mesh=mesh,
        in_specs=placed,
        out_specs=(P("row", None), P("row", "col")),
        check_vma=False,
    )
```

```python
import functools
import math

import jax
import jax.numpy as jnp
from jax import lax
from jax.experimental import pallas as pl
from jax.experimental.pallas import tpu as pltpu
from jax.sharding import PartitionSpec as P

H = 16
NOPE = 128
ROPE = 64
VDIM = 128
LATENT = 512
QK = NOPE + ROPE
HEAD_UP = NOPE + VDIM
LANES = 128
TAIL = 16
HIDDEN_SCORE = -1e30
VMEM_LIMIT = 24 * 1024 * 1024
PREPARE_LIMIT = 12 * 1024 * 1024
ASSEMBLE_LIMIT = 12 * 1024 * 1024
SUBLANES = 16
LOG2_SCALE = math.log2(math.e) / math.sqrt(QK)
NT = (((1,), (1,)), ((), ()))


def exchange(x, axis, step):
    count = lax.axis_size(axis)
    return lax.ppermute(x, axis, [(i, i ^ step) for i in range(count)])


def rotate(x, axis, step):
    count = lax.axis_size(axis)
    return lax.ppermute(x, axis, [(i, (i + step) % count) for i in range(count)])


def rows_of(ref, index, size):
    return ref[pl.ds(pl.multiple_of(index * size, size), size), :]


def prepare_kernel(
    offset_ref, table_hbm, len_hbm, queries_hbm, pool_hbm, up_hbm, *refs
):
    q_ref, keys_ref, up_ref, pages_ref, queries_ref, table_ref, len_ref, page_sem, sem = refs
    page_count, page_size, _ = pages_ref.shape
    query_rows = queries_ref.shape[0]

    scalar_copies = [
        pltpu.make_async_copy(source, target, sem.at[2 + i])
        for i, (source, target) in enumerate(
            ((table_hbm, table_ref), (len_hbm, len_ref))
        )
    ]
    for copy in scalar_copies:
        copy.start()

    queries_copy = pltpu.make_async_copy(queries_hbm, queries_ref, sem.at[0])
    up_copy = pltpu.make_async_copy(up_hbm, up_ref, sem.at[1])
    queries_copy.start()
    up_copy.start()
    for copy in scalar_copies:
        copy.wait()
    page_copies = [
        pltpu.make_async_copy(pool_hbm.at[table_ref[p]], pages_ref.at[p], page_sem.at[p])
        for p in range(page_count)
    ]
    for copy in page_copies:
        copy.start()
    first_query = offset_ref[0] + lax.axis_index("row") * query_rows
    first_key = lax.axis_index("col") * page_count * page_size

    slot = lax.broadcasted_iota(jnp.int32, (page_size, query_rows), 0)
    query_pos = first_query + lax.broadcasted_iota(jnp.int32, (page_size, query_rows), 1)
    for p in range(page_count):
        page_copies[p].wait()
        rows = pl.ds(p * page_size, page_size)
        page = pages_ref[p]
        keys_ref[rows, :LATENT] = page[:, :LATENT]
        keys_ref[rows, LATENT : LATENT + LANES] = jnp.concatenate(
            [page[:, LATENT:], jnp.zeros((page_size, LANES - ROPE), jnp.bfloat16)], axis=1
        )
        seen = (slot < len_ref[p]) & (first_key + p * page_size + slot <= query_pos)
        keys_ref[rows, LATENT + LANES :] = jnp.where(seen, 0.0, HIDDEN_SCORE).astype(jnp.bfloat16)

    eye = (
        lax.broadcasted_iota(jnp.int32, (query_rows, query_rows), 0)
        == lax.broadcasted_iota(jnp.int32, (query_rows, query_rows), 1)
    ).astype(jnp.bfloat16)
    queries_copy.wait()
    up_copy.wait()
    for h in range(H):
        rows = pl.ds(h * query_rows, query_rows)
        q_nope = queries_ref[:, h * QK : h * QK + NOPE]
        up_k = up_ref[:, h * HEAD_UP : h * HEAD_UP + NOPE]
        absorbed = lax.dot_general(q_nope, up_k, NT, preferred_element_type=jnp.float32)
        q_ref[rows, :LATENT] = absorbed.astype(jnp.bfloat16)
        q_rope = queries_ref[:, h * QK + NOPE : (h + 1) * QK]
        q_ref[rows, LATENT : LATENT + LANES] = jnp.concatenate(
            [q_rope, jnp.zeros((query_rows, LANES - ROPE), jnp.bfloat16)], axis=1
        )
        q_ref[rows, LATENT + LANES :] = eye


def cut_kernel(chips, gate_hbm, unit_hbm, down_hbm, *refs):
    shares, (share_sem,) = refs[:chips], refs[chips:]
    share = shares[0].shape[0] // 3
    units = gate_hbm.shape[0]
    chip_index = lax.axis_index("row") // 2
    share_copies = []
    for step in range(chips):
        at = share_start(chip_index ^ step, share, units)
        rows = pl.ds(pl.multiple_of(at, SUBLANES), share)
        for i, source in enumerate((gate_hbm, unit_hbm, down_hbm)):
            target = shares[step].at[pl.ds(i * share, share), :]
            share_copies.append(
                pltpu.make_async_copy(source.at[rows, :], target, share_sem.at[3 * step + i])
            )
    for copy in share_copies:
        copy.start()
    for copy in share_copies:
        copy.wait()


def cut(by_unit, chips, share):
    hbm = pl.BlockSpec(memory_space=pltpu.HBM)
    return pl.pallas_call(
        functools.partial(cut_kernel, chips),
        out_shape=[pltpu.VMEM((3 * share, by_unit[0].shape[1]), jnp.bfloat16)] * chips,
        in_specs=[hbm] * 3,
        out_specs=[pl.BlockSpec(memory_space=pltpu.VMEM)] * chips,
        scratch_shapes=[pltpu.SemaphoreType.DMA((3 * chips,))],
        compiler_params=pltpu.CompilerParams(vmem_limit_bytes=PREPARE_LIMIT),
        cost_estimate=pl.CostEstimate(flops=0, bytes_accessed=0, transcendentals=0),
        name="cut",
    )(*[pltpu.with_memory_space_constraint(x, pltpu.HBM) for x in by_unit])


def share_start(chip, share, units):
    return jnp.minimum(chip * share, units - share)


def prepare(block_table, page_len, group_offset, queries, latent_pool, latent_up):
    query_rows = queries.shape[0]
    page_count, page_size, cache_width = latent_pool.shape
    keys = page_count * page_size
    width = LATENT + LANES + query_rows
    vmem = pl.BlockSpec(memory_space=pltpu.VMEM)
    hbm = pl.BlockSpec(memory_space=pltpu.HBM)
    sources = (
        block_table, page_len, queries, latent_pool, latent_up
    )
    out = pl.pallas_call(
        prepare_kernel,
        out_shape=[
            pltpu.VMEM((H * query_rows, width), jnp.bfloat16),
            pltpu.VMEM((keys, width), jnp.bfloat16),
            pltpu.VMEM(latent_up.shape, jnp.bfloat16),
        ],
        in_specs=[pl.BlockSpec(memory_space=pltpu.SMEM)] + [hbm] * len(sources),
        out_specs=[vmem] * 3,
        scratch_shapes=[
            pltpu.VMEM((page_count, page_size, cache_width), jnp.bfloat16),
            pltpu.VMEM(queries.shape, jnp.bfloat16),
            pltpu.SMEM(block_table.shape, jnp.int32),
            pltpu.SMEM(page_len.shape, jnp.int32),
            pltpu.SemaphoreType.DMA((page_count,)),
            pltpu.SemaphoreType.DMA((4,)),
        ],
        compiler_params=pltpu.CompilerParams(vmem_limit_bytes=PREPARE_LIMIT),
        cost_estimate=pl.CostEstimate(flops=0, bytes_accessed=0, transcendentals=0),
        name="prepare",
    )(group_offset, *[pltpu.with_memory_space_constraint(x, pltpu.HBM) for x in sources])
    return out


def attend_kernel(step, groups, q_ref, keys_ref, up_ref, out_ref):
    heads_here = H // groups
    query_rows = q_ref.shape[0] // H
    group = lax.rem(lax.axis_index("col") + step, groups)
    q_rows = rows_of(q_ref, group, heads_here * query_rows)
    scores = lax.dot_general(q_rows, keys_ref[...], NT, preferred_element_type=jnp.float32)
    row_max = jnp.max(scores, axis=1, keepdims=True)
    weights = jnp.exp2((scores - row_max) * LOG2_SCALE)
    totals = jnp.sum(weights, axis=1, keepdims=True)
    context = jnp.dot(
        weights.astype(jnp.bfloat16), keys_ref[:, :LATENT], preferred_element_type=jnp.float32
    )
    context = (context / totals).astype(jnp.bfloat16)
    log_sum = row_max * LOG2_SCALE + jnp.log2(totals)
    tail = []
    for j in range(heads_here):
        own = slice(j * query_rows, (j + 1) * query_rows)
        at = pl.multiple_of((group * heads_here + j) * HEAD_UP + NOPE, LANES)
        up_v = up_ref[:, pl.ds(at, VDIM)]
        mixed = jnp.dot(context[own], up_v, preferred_element_type=jnp.float32)
        out_ref[:query_rows, j * VDIM : (j + 1) * VDIM] = mixed.astype(jnp.bfloat16)
        wide = jnp.broadcast_to(log_sum[own], (query_rows, LANES))
        tail.append(jnp.transpose(wide)[:1])
    tail = jnp.concatenate(tail, axis=1)
    high = tail.astype(jnp.bfloat16)
    rest = tail - high.astype(jnp.float32)
    middle = rest.astype(jnp.bfloat16)
    low = (rest - middle.astype(jnp.float32)).astype(jnp.bfloat16)
    parts = [high.astype(jnp.float32), middle.astype(jnp.float32), low.astype(jnp.float32)]
    parts.append(jnp.zeros((TAIL - 3, tail.shape[1]), jnp.float32))
    out_ref[query_rows:, :] = jnp.concatenate(parts, axis=0).astype(jnp.bfloat16)


def attend(step, groups, q, keys, latent_up):
    query_rows = q.shape[0] // H
    heads_here = H // groups
    vmem = pl.BlockSpec(memory_space=pltpu.VMEM)
    return pl.pallas_call(
        functools.partial(attend_kernel, step, groups),
        out_shape=jax.ShapeDtypeStruct((query_rows + TAIL, heads_here * VDIM), jnp.bfloat16),
        in_specs=[vmem, vmem, vmem],
        out_specs=vmem,
        compiler_params=pltpu.CompilerParams(vmem_limit_bytes=VMEM_LIMIT),
        cost_estimate=pl.CostEstimate(
            flops=7 * heads_here * query_rows * keys.shape[0] * (keys.shape[1] + LATENT) // 5,
            bytes_accessed=4 * 1024 * 1024,
            transcendentals=heads_here * query_rows * keys.shape[0],
        ),
        name="attend",
    )(q, keys, latent_up)


def project_kernel(groups, weight_ref, *refs):
    parts, outs = refs[:groups], refs[groups:]
    query_rows = outs[0].shape[0]
    width = outs[0].shape[1]
    heads_here = parts[0].shape[1] // VDIM
    col_index = lax.axis_index("col")
    mixed = []
    for j in range(heads_here):
        lanes = slice(j * VDIM, (j + 1) * VDIM)
        logs = []
        for part in parts:
            tail = part[query_rows:, lanes].astype(jnp.float32)
            line = tail[0:1] + tail[1:2] + tail[2:3]
            logs.append(jnp.transpose(jnp.broadcast_to(line, (LANES, query_rows))))
        top = functools.reduce(jnp.maximum, logs)
        scales = [jnp.exp2(v - top) for v in logs]
        total = functools.reduce(jnp.add, scales)
        value = functools.reduce(
            jnp.add, [s * part[:query_rows, lanes].astype(jnp.float32) for s, part in zip(scales, parts)]
        )
        mixed.append((value / total).astype(jnp.bfloat16))
    mixed = jnp.concatenate(mixed, axis=1)
    for step in range(groups):
        at = pl.multiple_of(lax.rem(col_index + step, groups) * width, width)
        columns = weight_ref[:, pl.ds(at, width)]
        outs[step][...] = jnp.dot(mixed, columns, preferred_element_type=jnp.float32).astype(
            jnp.bfloat16
        )


def project(parts, output_weight, query_rows):
    groups = len(parts)
    vmem = pl.BlockSpec(memory_space=pltpu.VMEM)
    width = output_weight.shape[1] // groups
    return pl.pallas_call(
        functools.partial(project_kernel, groups),
        out_shape=[jax.ShapeDtypeStruct((query_rows, width), jnp.bfloat16)] * groups,
        in_specs=[vmem] * (1 + groups),
        out_specs=[vmem] * groups,
        compiler_params=pltpu.CompilerParams(vmem_limit_bytes=32 * 1024 * 1024),
        name="project",
    )(output_weight, *parts)


def assemble_kernel(chips, groups, *refs):
    blocks, refs = refs[: 2 * chips], refs[2 * chips :]
    pieces, (in_ref, down_ref, attended_ref, sem) = refs[:groups], refs[groups:]
    depth = blocks[0].shape[1]
    width = pieces[0].shape[1]
    share = down_ref.shape[0]
    col_index = lax.axis_index("col")
    row_index = lax.axis_index("row")
    copies = []
    for core_step in range(2):
        for step in range(chips):
            number = core_step * chips + step
            at = (row_index ^ (2 * step + core_step)) * depth
            chunk, rest = at // width, lax.rem(at, width)
            arrives = lax.rem(col_index + groups - chunk, groups)
            leaves = lax.rem(chunk + groups - col_index, groups)
            for i, (ref, place, first, rows) in enumerate(
                ((in_ref, arrives, 0, 2 * share), (down_ref, leaves, 2 * share, share))
            ):
                lanes = pl.ds(pl.multiple_of(place * width + rest, depth), depth)
                source = blocks[number].at[pl.ds(first, rows), :]
                copies.append(
                    pltpu.make_async_copy(source, ref.at[:, lanes], sem.at[2 * number + i])
                )
    for copy in copies:
        copy.start()
    for s in range(groups):
        at = pl.multiple_of(lax.rem(col_index + groups - s, groups) * width, width)
        attended_ref[:, pl.ds(at, width)] = pieces[s][...]
    for copy in copies:
        copy.wait()


def assemble(blocks, pieces):
    rows, depth = blocks[0].shape
    share = rows // 3
    query_rows, width = pieces[0].shape
    model = depth * len(blocks)
    vmem = pl.BlockSpec(memory_space=pltpu.VMEM)
    return pl.pallas_call(
        functools.partial(assemble_kernel, len(blocks) // 2, len(pieces)),
        out_shape=[
            pltpu.VMEM((2 * share, model), jnp.bfloat16),
            pltpu.VMEM((share, model), jnp.bfloat16),
            jax.ShapeDtypeStruct((query_rows, model), jnp.bfloat16),
        ],
        in_specs=[vmem] * (len(blocks) + len(pieces)),
        out_specs=[vmem] * 3,
        scratch_shapes=[pltpu.SemaphoreType.DMA((2 * len(blocks),))],
        compiler_params=pltpu.CompilerParams(vmem_limit_bytes=ASSEMBLE_LIMIT),
        cost_estimate=pl.CostEstimate(
            flops=0, bytes_accessed=8 * rows * model, transcendentals=0
        ),
        name="assemble",
    )(*[pltpu.with_memory_space_constraint(block, pltpu.VMEM) for block in blocks], *pieces)


def gate_up(tokens, weights):
    together = jnp.concatenate(tokens, axis=1) if len(tokens) > 1 else tokens[0]
    sums = lax.dot_general(together, weights, NT, preferred_element_type=jnp.float32)
    squares = 0.0
    for token in tokens:
        wide = token.astype(jnp.float32)
        squares = squares + jnp.sum(wide * wide, axis=1, keepdims=True)
    return sums, squares


def feed_first_kernel(order, in_ref, *refs):
    sides, (sums_ref, squares_ref) = refs[:-2], refs[-2:]
    count = len(sides) // len(order)
    tokens = [
        join_rows(sides[i * count : (i + 1) * count], bits) for i, bits in enumerate(order)
    ]
    columns = sum(token.shape[1] for token in tokens)
    sums_ref[...], squares_ref[...] = gate_up(tokens, in_ref[:, :columns])


def feed_first(weights, tokens, order):
    rows, width = sum(side.shape[0] for side in tokens[0]), tokens[0][0].shape[1]
    sides = [side for token in tokens for side in token]
    vmem = pl.BlockSpec(memory_space=pltpu.VMEM)
    return pl.pallas_call(
        functools.partial(feed_first_kernel, order),
        out_shape=[
            pltpu.VMEM((rows, weights.shape[0]), jnp.float32),
            pltpu.VMEM((rows, 1), jnp.float32),
        ],
        in_specs=[vmem] * (1 + len(sides)),
        out_specs=[vmem] * 2,
        compiler_params=pltpu.CompilerParams(vmem_limit_bytes=VMEM_LIMIT),
        cost_estimate=pl.CostEstimate(
            flops=4 * rows * width * len(tokens) * weights.shape[0],
            bytes_accessed=1024 * 1024,
            transcendentals=0,
        ),
        name="feed_first",
    )(weights, *sides)


def feed_kernel(groups, chips, units, order, in_ref, down_ref, sums_ref, squares_ref, *refs):
    sides, refs = refs[: -2 * groups - 1], refs[-2 * groups - 1 :]
    keeps, sends, (active_ref,) = refs[:groups], refs[groups : 2 * groups], refs[2 * groups :]
    token = join_rows(sides, order[-1])
    rows, width = token.shape
    share, model = down_ref.shape
    query_rows = rows // chips
    sums, squares = gate_up([token], in_ref[:, model - width :])
    sums = sums + sums_ref[...]
    scale = lax.rsqrt((squares + squares_ref[...]) / model + 1e-06)
    gate = sums[:, :share] * scale
    active = gate / (1.0 + jnp.exp(-gate)) * (sums[:, share:] * scale)
    chip_index = lax.axis_index("row") // 2
    repeated = chip_index * share - share_start(chip_index, share, units)
    unit = lax.broadcasted_iota(jnp.int32, active.shape, 1)
    active_ref[...] = jnp.where(unit < repeated, 0.0, active).astype(jnp.bfloat16)
    for s in range(groups):
        out = jnp.dot(
            active_ref[...],
            down_ref[:, s * width : (s + 1) * width],
            preferred_element_type=jnp.float32,
        ).astype(jnp.bfloat16)
        kept, sent = halves(order[s], chips)
        for ref, steps in ((keeps[s], kept), (sends[s], sent)):
            for i, step in enumerate(steps):
                ref[i * query_rows : (i + 1) * query_rows, :] = out[
                    step * query_rows : (step + 1) * query_rows
                ]


def halves(bits, chips):
    if not bits:
        return [0], []
    return [s for s in range(chips) if not s & bits[0]], [s for s in range(chips) if s & bits[0]]


def feed(weights, down, partial, token, units, chips, order):
    rows, width = sum(side.shape[0] for side in token), token[0].shape[1]
    share, model = down.shape
    groups = model // width
    vmem = pl.BlockSpec(memory_space=pltpu.VMEM)
    kept, sent = halves(order[0], chips)
    query_rows = rows // chips
    shapes = [
        jax.ShapeDtypeStruct((max(len(steps), 1) * query_rows, width), jnp.bfloat16)
        for steps in (kept, sent)
    ]
    return pl.pallas_call(
        functools.partial(feed_kernel, groups, chips, units, order),
        out_shape=[shapes[0]] * groups + [shapes[1]] * groups,
        in_specs=[vmem] * (4 + len(token)),
        out_specs=[vmem] * (2 * groups),
        scratch_shapes=[pltpu.VMEM((rows, share), jnp.bfloat16)],
        compiler_params=pltpu.CompilerParams(vmem_limit_bytes=VMEM_LIMIT),
        cost_estimate=pl.CostEstimate(
            flops=2 * rows * model * share, bytes_accessed=1024 * 1024, transcendentals=0
        ),
        name="feed",
    )(weights, down, *partial, *token)


def gather_rows(block, bits, got):
    sides = [block, got]
    for bit in bits[1:]:
        block = jnp.concatenate(sides, axis=0)
        sides = [block, exchange(block, "row", 2 * bit)]
    return sides


def join_rows(sides, bits):
    steps = [0]
    for bit in bits:
        steps = steps + [s ^ bit for s in steps]
    rows = sides[0].shape[0] * len(sides) // len(steps)
    each = [side[at : at + rows, :] for side in sides for at in range(0, side.shape[0], rows)]
    return jnp.concatenate([each[steps.index(s)] for s in sorted(steps)], axis=0)


def sum_rows(kept, got, bits, query_rows):
    kept = kept.astype(jnp.float32) + got.astype(jnp.float32)
    for i, bit in enumerate(bits[1:], 1):
        left = [s for s in range(1 << len(bits)) if not any(s & b for b in bits[:i])]
        stays, goes = [
            jnp.concatenate(
                [
                    kept[n * query_rows : (n + 1) * query_rows]
                    for n, s in enumerate(left)
                    if bool(s & bit) == away
                ],
                axis=0,
            )
            for away in (False, True)
        ]
        kept = stays + exchange(goes.astype(jnp.bfloat16), "row", 2 * bit).astype(jnp.float32)
    return kept


def on_device(
    queries,
    latent_pool,
    block_table,
    page_len,
    group_offset,
    hidden,
    latent_up,
    output_weight,
    gate_weight,
    up_weight,
    down_weight,
):
    cols = lax.axis_size("col")
    chips = lax.axis_size("row") // 2
    col_index = lax.axis_index("col")
    query_rows, model = hidden.shape
    depth, units = gate_weight.shape
    by_unit = (gate_weight.T, up_weight.T, down_weight)
    if units % SUBLANES:
        by_unit = [jnp.pad(w, ((0, -units % SUBLANES), (0, 0))) for w in by_unit]
        units = by_unit[0].shape[0]
    share = -(-units // (chips * SUBLANES)) * SUBLANES
    width = model // cols

    shares = cut(by_unit, chips, share)
    q, keys, up_here = prepare(
        block_table, page_len, group_offset, queries, latent_pool, latent_up
    )
    early = range(1, chips // 2 + 1)
    late = range(chips // 2 + 1, chips)
    blocks = {s: exchange(shares[s], "row", 2 * s) for s in early}
    swapped = {0: exchange(shares[0], "row", 1)}

    payloads = [attend(s, cols, q, keys, up_here) for s in range(cols)]
    payloads[0], last = lax.optimization_barrier((payloads[0], [shares[s] for s in late]))
    parts = [payloads[0]] + [rotate(payloads[s], "col", s) for s in range(1, cols)]
    late_blocks = {s: exchange(share_out, "row", 2 * s) for s, share_out in zip(late, last)}
    terms = project(parts, output_weight, query_rows)
    terms, swapped, blocks = lax.optimization_barrier((terms, swapped, blocks))
    blocks.update(late_blocks)
    for s in early:
        swapped[s] = exchange(blocks[s], "row", 1)
    here = lax.dynamic_slice_in_dim(hidden, col_index * width, width, 1).astype(jnp.float32)
    here = here + terms[0].astype(jnp.float32)
    for s in range(1, cols):
        here = here + rotate(terms[s], "col", s).astype(jnp.float32)
    here = here.astype(jnp.bfloat16)
    here, swapped = lax.optimization_barrier((here, swapped))

    rising = [1 << i for i in range(chips.bit_length() - 1)]
    order = [rising if s % 2 == 0 else rising[::-1] for s in range(cols)]
    pieces = [here] + [rotate(here, "col", s) for s in range(1, cols)]
    got = [exchange(pieces[s], "row", 2 * order[s][0]) for s in range(cols)]
    got, blocks = lax.optimization_barrier((got, blocks))
    for s in late:
        swapped[s] = exchange(blocks[s], "row", 1)
    blocks[0] = shares[0]
    blocks = [blocks[s] for s in range(chips)] + [swapped[s] for s in range(chips)]
    tokens = [gather_rows(pieces[s], order[s], got[s]) for s in range(cols)]
    weights, down, attended = assemble(blocks, pieces)
    partial = feed_first(weights, tokens[:-1], order[:-1])
    out = feed(weights, down, partial, tokens[-1], units, chips, order)
    total = here.astype(jnp.float32)
    outward = range(cols - 1, 0, -1)
    got = {s: exchange(out[cols + s], "row", 2 * order[s][0]) for s in outward}
    got[0] = exchange(out[cols], "row", 2 * order[0][0])
    terms = {s: sum_rows(out[s], got[s], order[s], query_rows) for s in outward}
    for s in outward:
        total = total + rotate(terms[s].astype(jnp.bfloat16), "col", s).astype(jnp.float32)
    total = total + sum_rows(out[0], got[0], order[0], query_rows)
    return (attended, total.astype(jnp.bfloat16))


def solution(mesh):
    placed = (
        P("row", None),
        P("col", None, None),
        P("col"),
        P("col"),
        P(),
        P("row", None),
        P(),
        P("col", None),
        P("row", "col"),
        P("row", "col"),
        P("col", "row"),
    )
    return jax.shard_map(
        on_device,
        mesh=mesh,
        in_specs=placed,
        out_specs=(P("row", None), P("row", "col")),
        check_vma=False,
    )
```

```python
import functools
import math

import jax
import jax.numpy as jnp
from jax import lax
from jax.experimental import pallas as pl
from jax.experimental.pallas import tpu as pltpu
from jax.sharding import PartitionSpec as P

H = 16
NOPE = 128
ROPE = 64
VDIM = 128
LATENT = 512
QK = NOPE + ROPE
HEAD_UP = NOPE + VDIM
LANES = 128
TAIL = 16
HIDDEN_SCORE = -1e30
VMEM_LIMIT = 24 * 1024 * 1024
PREPARE_LIMIT = 12 * 1024 * 1024
ASSEMBLE_LIMIT = 12 * 1024 * 1024
SUBLANES = 16
UP_PARTS = 4
LOG2_SCALE = math.log2(math.e) / math.sqrt(QK)
NT = (((1,), (1,)), ((), ()))


def exchange(x, axis, step):
    count = lax.axis_size(axis)
    return lax.ppermute(x, axis, [(i, i ^ step) for i in range(count)])


def rotate(x, axis, step):
    count = lax.axis_size(axis)
    return lax.ppermute(x, axis, [(i, (i + step) % count) for i in range(count)])


def rows_of(ref, index, size):
    return ref[pl.ds(pl.multiple_of(index * size, size), size), :]


def prepare_kernel(
    offset_ref, table_hbm, len_hbm, queries_hbm, pool_hbm, up_hbm, *refs
):
    q_ref, keys_ref, up_ref, pages_ref, queries_ref, table_ref, len_ref, page_sem, up_sem, sem = refs
    page_count, page_size, _ = pages_ref.shape
    query_rows = queries_ref.shape[0]

    scalar_copies = [
        pltpu.make_async_copy(source, target, sem.at[2 + i])
        for i, (source, target) in enumerate(
            ((table_hbm, table_ref), (len_hbm, len_ref))
        )
    ]
    for copy in scalar_copies:
        copy.start()

    queries_copy = pltpu.make_async_copy(queries_hbm, queries_ref, sem.at[0])
    part = up_ref.shape[0] // UP_PARTS
    up_copies = [
        pltpu.make_async_copy(
            up_hbm.at[pl.ds(i * part, part), :], up_ref.at[pl.ds(i * part, part), :], up_sem.at[i]
        )
        for i in range(UP_PARTS)
    ]
    queries_copy.start()
    for copy in up_copies:
        copy.start()
    for copy in scalar_copies:
        copy.wait()
    page_copies = [
        pltpu.make_async_copy(pool_hbm.at[table_ref[p]], pages_ref.at[p], page_sem.at[p])
        for p in range(page_count)
    ]
    for copy in page_copies:
        copy.start()
    first_query = offset_ref[0] + lax.axis_index("row") * query_rows
    first_key = lax.axis_index("col") * page_count * page_size

    slot = lax.broadcasted_iota(jnp.int32, (page_size, query_rows), 0)
    query_pos = first_query + lax.broadcasted_iota(jnp.int32, (page_size, query_rows), 1)
    for p in range(page_count):
        page_copies[p].wait()
        rows = pl.ds(p * page_size, page_size)
        page = pages_ref[p]
        keys_ref[rows, :LATENT] = page[:, :LATENT]
        keys_ref[rows, LATENT : LATENT + LANES] = jnp.concatenate(
            [page[:, LATENT:], jnp.zeros((page_size, LANES - ROPE), jnp.bfloat16)], axis=1
        )
        seen = (slot < len_ref[p]) & (first_key + p * page_size + slot <= query_pos)
        keys_ref[rows, LATENT + LANES :] = jnp.where(seen, 0.0, HIDDEN_SCORE).astype(jnp.bfloat16)

    eye = (
        lax.broadcasted_iota(jnp.int32, (query_rows, query_rows), 0)
        == lax.broadcasted_iota(jnp.int32, (query_rows, query_rows), 1)
    ).astype(jnp.bfloat16)
    queries_copy.wait()
    for copy in up_copies:
        copy.wait()
    for h in range(H):
        rows = pl.ds(h * query_rows, query_rows)
        q_nope = queries_ref[:, h * QK : h * QK + NOPE]
        up_k = up_ref[:, h * HEAD_UP : h * HEAD_UP + NOPE]
        absorbed = lax.dot_general(q_nope, up_k, NT, preferred_element_type=jnp.float32)
        q_ref[rows, :LATENT] = absorbed.astype(jnp.bfloat16)
        q_rope = queries_ref[:, h * QK + NOPE : (h + 1) * QK]
        q_ref[rows, LATENT : LATENT + LANES] = jnp.concatenate(
            [q_rope, jnp.zeros((query_rows, LANES - ROPE), jnp.bfloat16)], axis=1
        )
        q_ref[rows, LATENT + LANES :] = eye


def cut_kernel(chips, gate_hbm, unit_hbm, down_hbm, *refs):
    shares, (share_sem,) = refs[:chips], refs[chips:]
    share = shares[0].shape[0] // 3
    units = gate_hbm.shape[0]
    chip_index = lax.axis_index("row") // 2
    share_copies = []
    for step in range(chips):
        at = share_start(chip_index ^ step, share, units)
        rows = pl.ds(pl.multiple_of(at, SUBLANES), share)
        for i, source in enumerate((gate_hbm, unit_hbm, down_hbm)):
            target = shares[step].at[pl.ds(i * share, share), :]
            share_copies.append(
                pltpu.make_async_copy(source.at[rows, :], target, share_sem.at[3 * step + i])
            )
    for copy in share_copies:
        copy.start()
    for copy in share_copies:
        copy.wait()


def cut(by_unit, chips, share):
    hbm = pl.BlockSpec(memory_space=pltpu.HBM)
    return pl.pallas_call(
        functools.partial(cut_kernel, chips),
        out_shape=[pltpu.VMEM((3 * share, by_unit[0].shape[1]), jnp.bfloat16)] * chips,
        in_specs=[hbm] * 3,
        out_specs=[pl.BlockSpec(memory_space=pltpu.VMEM)] * chips,
        scratch_shapes=[pltpu.SemaphoreType.DMA((3 * chips,))],
        compiler_params=pltpu.CompilerParams(vmem_limit_bytes=PREPARE_LIMIT),
        cost_estimate=pl.CostEstimate(flops=0, bytes_accessed=0, transcendentals=0),
        name="cut",
    )(*[pltpu.with_memory_space_constraint(x, pltpu.HBM) for x in by_unit])


def share_start(chip, share, units):
    return jnp.minimum(chip * share, units - share)


def prepare(block_table, page_len, group_offset, queries, latent_pool, latent_up):
    query_rows = queries.shape[0]
    page_count, page_size, cache_width = latent_pool.shape
    keys = page_count * page_size
    width = LATENT + LANES + query_rows
    vmem = pl.BlockSpec(memory_space=pltpu.VMEM)
    hbm = pl.BlockSpec(memory_space=pltpu.HBM)
    sources = (
        block_table, page_len, queries, latent_pool, latent_up
    )
    out = pl.pallas_call(
        prepare_kernel,
        out_shape=[
            pltpu.VMEM((H * query_rows, width), jnp.bfloat16),
            pltpu.VMEM((keys, width), jnp.bfloat16),
            pltpu.VMEM(latent_up.shape, jnp.bfloat16),
        ],
        in_specs=[pl.BlockSpec(memory_space=pltpu.SMEM)] + [hbm] * len(sources),
        out_specs=[vmem] * 3,
        scratch_shapes=[
            pltpu.VMEM((page_count, page_size, cache_width), jnp.bfloat16),
            pltpu.VMEM(queries.shape, jnp.bfloat16),
            pltpu.SMEM(block_table.shape, jnp.int32),
            pltpu.SMEM(page_len.shape, jnp.int32),
            pltpu.SemaphoreType.DMA((page_count,)),
            pltpu.SemaphoreType.DMA((UP_PARTS,)),
            pltpu.SemaphoreType.DMA((4,)),
        ],
        compiler_params=pltpu.CompilerParams(vmem_limit_bytes=PREPARE_LIMIT),
        cost_estimate=pl.CostEstimate(flops=0, bytes_accessed=0, transcendentals=0),
        name="prepare",
    )(group_offset, *[pltpu.with_memory_space_constraint(x, pltpu.HBM) for x in sources])
    return out


def attend_kernel(step, groups, q_ref, keys_ref, up_ref, out_ref):
    heads_here = H // groups
    query_rows = q_ref.shape[0] // H
    group = lax.rem(lax.axis_index("col") + step, groups)
    q_rows = rows_of(q_ref, group, heads_here * query_rows)
    scores = lax.dot_general(q_rows, keys_ref[...], NT, preferred_element_type=jnp.float32)
    row_max = jnp.max(scores, axis=1, keepdims=True)
    weights = jnp.exp2((scores - row_max) * LOG2_SCALE)
    totals = jnp.sum(weights, axis=1, keepdims=True)
    context = jnp.dot(
        weights.astype(jnp.bfloat16), keys_ref[:, :LATENT], preferred_element_type=jnp.float32
    )
    context = (context / totals).astype(jnp.bfloat16)
    log_sum = row_max * LOG2_SCALE + jnp.log2(totals)
    tail = []
    for j in range(heads_here):
        own = slice(j * query_rows, (j + 1) * query_rows)
        at = pl.multiple_of((group * heads_here + j) * HEAD_UP + NOPE, LANES)
        up_v = up_ref[:, pl.ds(at, VDIM)]
        mixed = jnp.dot(context[own], up_v, preferred_element_type=jnp.float32)
        out_ref[:query_rows, j * VDIM : (j + 1) * VDIM] = mixed.astype(jnp.bfloat16)
        wide = jnp.broadcast_to(log_sum[own], (query_rows, LANES))
        tail.append(jnp.transpose(wide)[:1])
    tail = jnp.concatenate(tail, axis=1)
    high = tail.astype(jnp.bfloat16)
    rest = tail - high.astype(jnp.float32)
    middle = rest.astype(jnp.bfloat16)
    low = (rest - middle.astype(jnp.float32)).astype(jnp.bfloat16)
    parts = [high.astype(jnp.float32), middle.astype(jnp.float32), low.astype(jnp.float32)]
    parts.append(jnp.zeros((TAIL - 3, tail.shape[1]), jnp.float32))
    out_ref[query_rows:, :] = jnp.concatenate(parts, axis=0).astype(jnp.bfloat16)


def attend(step, groups, q, keys, latent_up):
    query_rows = q.shape[0] // H
    heads_here = H // groups
    vmem = pl.BlockSpec(memory_space=pltpu.VMEM)
    return pl.pallas_call(
        functools.partial(attend_kernel, step, groups),
        out_shape=jax.ShapeDtypeStruct((query_rows + TAIL, heads_here * VDIM), jnp.bfloat16),
        in_specs=[vmem, vmem, vmem],
        out_specs=vmem,
        compiler_params=pltpu.CompilerParams(vmem_limit_bytes=VMEM_LIMIT),
        cost_estimate=pl.CostEstimate(
            flops=7 * heads_here * query_rows * keys.shape[0] * (keys.shape[1] + LATENT) // 5,
            bytes_accessed=4 * 1024 * 1024,
            transcendentals=heads_here * query_rows * keys.shape[0],
        ),
        name="attend",
    )(q, keys, latent_up)


def project_kernel(groups, weight_ref, *refs):
    parts, outs = refs[:groups], refs[groups:]
    query_rows = outs[0].shape[0]
    width = outs[0].shape[1]
    heads_here = parts[0].shape[1] // VDIM
    col_index = lax.axis_index("col")
    mixed = []
    for j in range(heads_here):
        lanes = slice(j * VDIM, (j + 1) * VDIM)
        logs = []
        for part in parts:
            tail = part[query_rows:, lanes].astype(jnp.float32)
            line = tail[0:1] + tail[1:2] + tail[2:3]
            logs.append(jnp.transpose(jnp.broadcast_to(line, (LANES, query_rows))))
        top = functools.reduce(jnp.maximum, logs)
        scales = [jnp.exp2(v - top) for v in logs]
        total = functools.reduce(jnp.add, scales)
        value = functools.reduce(
            jnp.add, [s * part[:query_rows, lanes].astype(jnp.float32) for s, part in zip(scales, parts)]
        )
        mixed.append((value / total).astype(jnp.bfloat16))
    mixed = jnp.concatenate(mixed, axis=1)
    for step in range(groups):
        at = pl.multiple_of(lax.rem(col_index + step, groups) * width, width)
        columns = weight_ref[:, pl.ds(at, width)]
        outs[step][...] = jnp.dot(mixed, columns, preferred_element_type=jnp.float32).astype(
            jnp.bfloat16
        )


def project(parts, output_weight, query_rows):
    groups = len(parts)
    vmem = pl.BlockSpec(memory_space=pltpu.VMEM)
    width = output_weight.shape[1] // groups
    return pl.pallas_call(
        functools.partial(project_kernel, groups),
        out_shape=[jax.ShapeDtypeStruct((query_rows, width), jnp.bfloat16)] * groups,
        in_specs=[vmem] * (1 + groups),
        out_specs=[vmem] * groups,
        compiler_params=pltpu.CompilerParams(vmem_limit_bytes=32 * 1024 * 1024),
        name="project",
    )(output_weight, *parts)


def assemble_kernel(chips, groups, *refs):
    blocks, refs = refs[: 2 * chips], refs[2 * chips :]
    pieces, (in_ref, down_ref, attended_ref, sem) = refs[:groups], refs[groups:]
    depth = blocks[0].shape[1]
    width = pieces[0].shape[1]
    share = down_ref.shape[0]
    col_index = lax.axis_index("col")
    row_index = lax.axis_index("row")
    copies = []
    for core_step in range(2):
        for step in range(chips):
            number = core_step * chips + step
            at = (row_index ^ (2 * step + core_step)) * depth
            chunk, rest = at // width, lax.rem(at, width)
            arrives = lax.rem(col_index + groups - chunk, groups)
            leaves = lax.rem(chunk + groups - col_index, groups)
            for i, (ref, place, first, rows) in enumerate(
                ((in_ref, arrives, 0, 2 * share), (down_ref, leaves, 2 * share, share))
            ):
                lanes = pl.ds(pl.multiple_of(place * width + rest, depth), depth)
                source = blocks[number].at[pl.ds(first, rows), :]
                copies.append(
                    pltpu.make_async_copy(source, ref.at[:, lanes], sem.at[2 * number + i])
                )
    for copy in copies:
        copy.start()
    for s in range(groups):
        at = pl.multiple_of(lax.rem(col_index + groups - s, groups) * width, width)
        attended_ref[:, pl.ds(at, width)] = pieces[s][...]
    for copy in copies:
        copy.wait()


def assemble(blocks, pieces):
    rows, depth = blocks[0].shape
    share = rows // 3
    query_rows, width = pieces[0].shape
    model = depth * len(blocks)
    vmem = pl.BlockSpec(memory_space=pltpu.VMEM)
    return pl.pallas_call(
        functools.partial(assemble_kernel, len(blocks) // 2, len(pieces)),
        out_shape=[
            pltpu.VMEM((2 * share, model), jnp.bfloat16),
            pltpu.VMEM((share, model), jnp.bfloat16),
            jax.ShapeDtypeStruct((query_rows, model), jnp.bfloat16),
        ],
        in_specs=[vmem] * (len(blocks) + len(pieces)),
        out_specs=[vmem] * 3,
        scratch_shapes=[pltpu.SemaphoreType.DMA((2 * len(blocks),))],
        compiler_params=pltpu.CompilerParams(vmem_limit_bytes=ASSEMBLE_LIMIT),
        cost_estimate=pl.CostEstimate(
            flops=0, bytes_accessed=8 * rows * model, transcendentals=0
        ),
        name="assemble",
    )(*[pltpu.with_memory_space_constraint(block, pltpu.VMEM) for block in blocks], *pieces)


def gate_up(tokens, weights):
    together = jnp.concatenate(tokens, axis=1) if len(tokens) > 1 else tokens[0]
    sums = lax.dot_general(together, weights, NT, preferred_element_type=jnp.float32)
    squares = 0.0
    for token in tokens:
        wide = token.astype(jnp.float32)
        squares = squares + jnp.sum(wide * wide, axis=1, keepdims=True)
    return sums, squares


def feed_first_kernel(order, in_ref, *refs):
    sides, (sums_ref, squares_ref) = refs[:-2], refs[-2:]
    count = len(sides) // len(order)
    tokens = [
        join_rows(sides[i * count : (i + 1) * count], bits) for i, bits in enumerate(order)
    ]
    columns = sum(token.shape[1] for token in tokens)
    sums_ref[...], squares_ref[...] = gate_up(tokens, in_ref[:, :columns])


def feed_first(weights, tokens, order):
    rows, width = sum(side.shape[0] for side in tokens[0]), tokens[0][0].shape[1]
    sides = [side for token in tokens for side in token]
    vmem = pl.BlockSpec(memory_space=pltpu.VMEM)
    return pl.pallas_call(
        functools.partial(feed_first_kernel, order),
        out_shape=[
            pltpu.VMEM((rows, weights.shape[0]), jnp.float32),
            pltpu.VMEM((rows, 1), jnp.float32),
        ],
        in_specs=[vmem] * (1 + len(sides)),
        out_specs=[vmem] * 2,
        compiler_params=pltpu.CompilerParams(vmem_limit_bytes=VMEM_LIMIT),
        cost_estimate=pl.CostEstimate(
            flops=4 * rows * width * len(tokens) * weights.shape[0],
            bytes_accessed=1024 * 1024,
            transcendentals=0,
        ),
        name="feed_first",
    )(weights, *sides)


def feed_kernel(groups, chips, units, order, in_ref, down_ref, sums_ref, squares_ref, *refs):
    sides, refs = refs[: -2 * groups - 1], refs[-2 * groups - 1 :]
    keeps, sends, (active_ref,) = refs[:groups], refs[groups : 2 * groups], refs[2 * groups :]
    token = join_rows(sides, order[-1])
    rows, width = token.shape
    share, model = down_ref.shape
    query_rows = rows // chips
    sums, squares = gate_up([token], in_ref[:, model - width :])
    sums = sums + sums_ref[...]
    scale = lax.rsqrt((squares + squares_ref[...]) / model + 1e-06)
    gate = sums[:, :share] * scale
    active = gate / (1.0 + jnp.exp(-gate)) * (sums[:, share:] * scale)
    chip_index = lax.axis_index("row") // 2
    repeated = chip_index * share - share_start(chip_index, share, units)
    unit = lax.broadcasted_iota(jnp.int32, active.shape, 1)
    active_ref[...] = jnp.where(unit < repeated, 0.0, active).astype(jnp.bfloat16)
    for s in range(groups):
        out = jnp.dot(
            active_ref[...],
            down_ref[:, s * width : (s + 1) * width],
            preferred_element_type=jnp.float32,
        ).astype(jnp.bfloat16)
        kept, sent = halves(order[s], chips)
        for ref, steps in ((keeps[s], kept), (sends[s], sent)):
            for i, step in enumerate(steps):
                ref[i * query_rows : (i + 1) * query_rows, :] = out[
                    step * query_rows : (step + 1) * query_rows
                ]


def halves(bits, chips):
    if not bits:
        return [0], []
    return [s for s in range(chips) if not s & bits[0]], [s for s in range(chips) if s & bits[0]]


def feed(weights, down, partial, token, units, chips, order):
    rows, width = sum(side.shape[0] for side in token), token[0].shape[1]
    share, model = down.shape
    groups = model // width
    vmem = pl.BlockSpec(memory_space=pltpu.VMEM)
    kept, sent = halves(order[0], chips)
    query_rows = rows // chips
    shapes = [
        jax.ShapeDtypeStruct((max(len(steps), 1) * query_rows, width), jnp.bfloat16)
        for steps in (kept, sent)
    ]
    return pl.pallas_call(
        functools.partial(feed_kernel, groups, chips, units, order),
        out_shape=[shapes[0]] * groups + [shapes[1]] * groups,
        in_specs=[vmem] * (4 + len(token)),
        out_specs=[vmem] * (2 * groups),
        scratch_shapes=[pltpu.VMEM((rows, share), jnp.bfloat16)],
        compiler_params=pltpu.CompilerParams(vmem_limit_bytes=VMEM_LIMIT),
        cost_estimate=pl.CostEstimate(
            flops=2 * rows * model * share, bytes_accessed=1024 * 1024, transcendentals=0
        ),
        name="feed",
    )(weights, down, *partial, *token)


def gather_rows(block, bits, got):
    sides = [block, got]
    for bit in bits[1:]:
        block = jnp.concatenate(sides, axis=0)
        sides = [block, exchange(block, "row", 2 * bit)]
    return sides


def join_rows(sides, bits):
    steps = [0]
    for bit in bits:
        steps = steps + [s ^ bit for s in steps]
    rows = sides[0].shape[0] * len(sides) // len(steps)
    each = [side[at : at + rows, :] for side in sides for at in range(0, side.shape[0], rows)]
    return jnp.concatenate([each[steps.index(s)] for s in sorted(steps)], axis=0)


def sum_rows(kept, got, bits, query_rows):
    kept = kept.astype(jnp.float32) + got.astype(jnp.float32)
    for i, bit in enumerate(bits[1:], 1):
        left = [s for s in range(1 << len(bits)) if not any(s & b for b in bits[:i])]
        stays, goes = [
            jnp.concatenate(
                [
                    kept[n * query_rows : (n + 1) * query_rows]
                    for n, s in enumerate(left)
                    if bool(s & bit) == away
                ],
                axis=0,
            )
            for away in (False, True)
        ]
        kept = stays + exchange(goes.astype(jnp.bfloat16), "row", 2 * bit).astype(jnp.float32)
    return kept


def on_device(
    queries,
    latent_pool,
    block_table,
    page_len,
    group_offset,
    hidden,
    latent_up,
    output_weight,
    gate_weight,
    up_weight,
    down_weight,
):
    cols = lax.axis_size("col")
    chips = lax.axis_size("row") // 2
    col_index = lax.axis_index("col")
    query_rows, model = hidden.shape
    depth, units = gate_weight.shape
    by_unit = (gate_weight.T, up_weight.T, down_weight)
    if units % SUBLANES:
        by_unit = [jnp.pad(w, ((0, -units % SUBLANES), (0, 0))) for w in by_unit]
        units = by_unit[0].shape[0]
    share = -(-units // (chips * SUBLANES)) * SUBLANES
    width = model // cols

    shares = cut(by_unit, chips, share)
    q, keys, up_here = prepare(
        block_table, page_len, group_offset, queries, latent_pool, latent_up
    )
    early = range(1, chips // 2 + 1)
    late = range(chips // 2 + 1, chips)
    blocks = {s: exchange(shares[s], "row", 2 * s) for s in early}
    swapped = {0: exchange(shares[0], "row", 1)}

    payloads = [attend(s, cols, q, keys, up_here) for s in range(cols)]
    payloads[0], last = lax.optimization_barrier((payloads[0], [shares[s] for s in late]))
    parts = [payloads[0]] + [rotate(payloads[s], "col", s) for s in range(1, cols)]
    late_blocks = {s: exchange(share_out, "row", 2 * s) for s, share_out in zip(late, last)}
    terms = project(parts, output_weight, query_rows)
    terms, swapped, blocks = lax.optimization_barrier((terms, swapped, blocks))
    blocks.update(late_blocks)
    for s in early:
        swapped[s] = exchange(blocks[s], "row", 1)
    here = lax.dynamic_slice_in_dim(hidden, col_index * width, width, 1).astype(jnp.float32)
    here = here + terms[0].astype(jnp.float32)
    for s in range(1, cols):
        here = here + rotate(terms[s], "col", s).astype(jnp.float32)
    here = here.astype(jnp.bfloat16)
    here, swapped = lax.optimization_barrier((here, swapped))

    rising = [1 << i for i in range(chips.bit_length() - 1)]
    order = [rising if s % 2 == 0 else rising[::-1] for s in range(cols)]
    pieces = [here] + [rotate(here, "col", s) for s in range(1, cols)]
    got = [exchange(pieces[s], "row", 2 * order[s][0]) for s in range(cols)]
    got, blocks = lax.optimization_barrier((got, blocks))
    for s in late:
        swapped[s] = exchange(blocks[s], "row", 1)
    blocks[0] = shares[0]
    blocks = [blocks[s] for s in range(chips)] + [swapped[s] for s in range(chips)]
    tokens = [gather_rows(pieces[s], order[s], got[s]) for s in range(cols)]
    weights, down, attended = assemble(blocks, pieces)
    partial = feed_first(weights, tokens[:-1], order[:-1])
    out = feed(weights, down, partial, tokens[-1], units, chips, order)
    total = here.astype(jnp.float32)
    outward = range(cols - 1, 0, -1)
    got = {s: exchange(out[cols + s], "row", 2 * order[s][0]) for s in outward}
    got[0] = exchange(out[cols], "row", 2 * order[0][0])
    terms = {s: sum_rows(out[s], got[s], order[s], query_rows) for s in outward}
    for s in outward:
        total = total + rotate(terms[s].astype(jnp.bfloat16), "col", s).astype(jnp.float32)
    total = total + sum_rows(out[0], got[0], order[0], query_rows)
    return (attended, total.astype(jnp.bfloat16))


def solution(mesh):
    placed = (
        P("row", None),
        P("col", None, None),
        P("col"),
        P("col"),
        P(),
        P("row", None),
        P(),
        P("col", None),
        P("row", "col"),
        P("row", "col"),
        P("col", "row"),
    )
    return jax.shard_map(
        on_device,
        mesh=mesh,
        in_specs=placed,
        out_specs=(P("row", None), P("row", "col")),
        check_vma=False,
    )
```
